512 devices in a mesh: section: 16 (over y, x), tm: 32 (over z, core).
Axes of the slice: x: 4, y: 4, z: 16, core: 2. Of those that a mesh axis runs over, the one named last changes fastest.
Arguments:
- series: bfloat16 [7, 4096, 1024], P(None, 'tm', 'section'), may hold values from -6 to 6
- query_key_value_weight: bfloat16 [16, 1024, 1536], P('section'), may hold values from -1.25 to 1.25, as said below
- output_weight: bfloat16 [16, 512, 1024], P('section'), may hold values from -0.25 to 0.25
- gain: float32 [16, 1024], P('section'), may hold values from 0.5 to 1.5
- readout_weight: float32 [16, 1024], P('section'), may hold values from -0.046875 to 0.046875
- dilation_block: int32 [64], replicated, may hold values from 0 to 1
- order: int32 [7], replicated, may hold values from 0 to 6, each once
Outputs:
- rul: float32 [7, 32, 128], P(None, 'tm', 'section')
The draws below stay inside these ranges and needn't reach their ends.
Inputs may be any that keep to these rules, and one draw needn't show every extreme that they name: `query_key_value_weight`: entries of order the inverse square root of 1024. `order`: A permutation of the slots.
All inputs are finite; a program needn't handle non-finite values.
Results may differ from the reference program's by a relative error of at most 0.025.
Values may be sent and summed in bfloat16 or wider, within the bound.
A program may use at most 64 MiB of HBM per device.

```python
import math
import jax
import jax.numpy as jnp
from jax import lax

D = 1024
HEADS_L = 4
HEADS_D = 4
HD = 64
ROWS = 128
MICRO = 7
WINDOW = 256
BLK = 64
LAYERS = 16
TILES = 32
SEQ = 4096
SHARD_BLOCKS = 2
SERIES_BLOCKS = 64


def draw_query_key_value_weight(key, part):
    width = (HEADS_L + HEADS_D) * HD
    shape = (LAYERS, D, 3 * width)
    base = jnp.clip(jax.random.normal(key, shape, jnp.float32), -6.0, 6.0) / math.sqrt(D)
    return base.astype(jnp.bfloat16)


def place_ends(drawn, own_key, low, high):
    longest = drawn.shape.index(max(drawn.shape))
    spots = []
    for shift in (0, 1):
        where = [jax.random.randint(jax.random.fold_in(own_key, axis), (), 0, length) for axis, length in enumerate(drawn.shape)]
        where[longest] = (where[longest] + shift) % drawn.shape[longest]
        spots.append(tuple(where))
    return drawn.at[spots[0]].set(low).at[spots[1]].set(high)


def steps_of(own_key, extent, split, least, largest):
    def one(dim, shards_of):
        heights = jax.random.uniform(jax.random.fold_in(jax.random.fold_in(own_key, 6), dim), (shards_of,), jnp.float32, least / len(split), largest / len(split))
        return jnp.repeat(jnp.exp(heights), extent[dim] // shards_of).reshape((-1,) + (1,) * (len(extent) - dim - 1))

    loudness = one(*split[0])
    for cut in split[1:]:
        loudness = loudness * one(*cut)
    return loudness


def noise(own_key, shape, deviation, reach, split=(), held_as=jnp.bfloat16):
    factor_of = steps_of(own_key, shape, split, -0.22, 0.18) if split else 1.0
    drawn = jax.random.normal(own_key, shape, jnp.float32) * deviation * factor_of
    return jnp.minimum(jnp.maximum(drawn, -reach), reach).astype(held_as)


def setup_inputs(seed: int = 0) -> dict:
    splits = jax.random.split(jax.random.key(seed), 8)
    series = noise(splits[0], (MICRO, SEQ, D), 1.0, 6.0, ((1, 32), (2, 16)))
    query_key_value_weight = draw_query_key_value_weight(jax.random.fold_in(splits[7], 71), 0)
    output_weight = noise(splits[2], (LAYERS, (HEADS_L + HEADS_D) * HD, D), ((HEADS_L + HEADS_D) * HD) ** -0.5, 0.25, ((0, 16),))
    gain = jnp.clip(1.0 + 0.1 * jax.random.normal(splits[3], (LAYERS, D), jnp.float32), 0.5, 1.5)
    readout_weight = noise(splits[4], (LAYERS, D), (D * LAYERS) ** -0.5, 0.046875, ((0, 16),), jnp.float32)
    dilation_block = place_ends(jax.random.randint(splits[5], (SERIES_BLOCKS,), 0, SHARD_BLOCKS), jax.random.fold_in(splits[5], 1), 0, SHARD_BLOCKS - 1).astype(jnp.int32)
    order = jax.random.permutation(splits[6], MICRO).astype(jnp.int32)
    return {"series": series, "query_key_value_weight": query_key_value_weight, "output_weight": output_weight, "gain": gain, "readout_weight": readout_weight, "dilation_block": dilation_block, "order": order}


EPSILON = 1e-05

def norm_rows(values):
    return values * lax.rsqrt(lax.optimization_barrier(jnp.mean(values * values, axis=-1, keepdims=True)) + EPSILON)

def soft_weights(scores, allowed):
    if allowed is not None:
        scores = jnp.where(allowed, scores, -1e+30)
    top_score = lax.optimization_barrier(jnp.max(scores, axis=-1, keepdims=True))
    raised = jnp.exp(scores - top_score)
    return (raised / lax.optimization_barrier(jnp.sum(raised, axis=-1, keepdims=True))).astype(jnp.bfloat16)

def reference(series, query_key_value_weight, output_weight, gain, readout_weight, dilation_block, order):
    local_width = HEADS_L * HD
    dilated_width = HEADS_D * HD
    head_width = local_width + dilated_width
    score_scale = HD ** (-0.5)
    highest = lax.Precision.HIGHEST
    shard_of = jnp.arange(SERIES_BLOCKS, dtype=jnp.int32) // SHARD_BLOCKS
    distant_shard = (shard_of + TILES - TILES // 2) % TILES
    block_numbers = (distant_shard * SHARD_BLOCKS + dilation_block).astype(jnp.int32)

    def layer_step(hidden, weights):
        weight_qkv, weight_out, norm_gain, read_vector = weights
        hidden_f = hidden.astype(jnp.float32)
        normed = (norm_rows(hidden_f) * norm_gain).astype(jnp.bfloat16)
        projected = jnp.dot(normed, weight_qkv, preferred_element_type=jnp.float32)
        query_cols = projected[:, :head_width]
        key_cols = projected[:, head_width:2 * head_width]
        value_cols = projected[:, 2 * head_width:]
        near_queries = query_cols[:, :local_width].reshape(SEQ, HEADS_L, HD)
        pad_zeros = jnp.zeros((WINDOW, HEADS_L, HD), jnp.float32)
        padded_keys = jnp.concatenate([pad_zeros, key_cols[:, :local_width].reshape(SEQ, HEADS_L, HD)], axis=0)
        padded_values = jnp.concatenate([pad_zeros, value_cols[:, :local_width].reshape(SEQ, HEADS_L, HD)], axis=0)

        def near_block(block_index):
            first_row = block_index * ROWS
            block_queries = lax.dynamic_slice_in_dim(near_queries, first_row, ROWS, 0)
            block_keys = lax.dynamic_slice_in_dim(padded_keys, first_row, ROWS + WINDOW, 0)
            block_values = lax.dynamic_slice_in_dim(padded_values, first_row, ROWS + WINDOW, 0)
            query_pos = first_row + jnp.arange(ROWS, dtype=jnp.int32)
            key_pos = first_row - WINDOW + jnp.arange(ROWS + WINDOW, dtype=jnp.int32)
            allowed = (key_pos[None, :] > query_pos[:, None] - WINDOW) & (key_pos[None, :] <= query_pos[:, None]) & (key_pos[None, :] >= 0)
            scores = jnp.einsum('qhd,khd->hqk', block_queries, block_keys, precision=highest) * score_scale
            weights_near = soft_weights(scores, allowed[None])
            block_out = jnp.einsum('hqk,khd->qhd', weights_near.astype(jnp.float32), block_values, precision=highest)
            return block_out.reshape(ROWS, local_width)
        near_out = lax.map(near_block, jnp.arange(TILES, dtype=jnp.int32)).reshape(SEQ, local_width)
        far_queries = query_cols[:, local_width:].reshape(SERIES_BLOCKS, BLK, HEADS_D, HD)
        own_keys = key_cols[:, local_width:].reshape(SERIES_BLOCKS, BLK, HEADS_D, HD)
        own_values = value_cols[:, local_width:].reshape(SERIES_BLOCKS, BLK, HEADS_D, HD)
        far_keys = jnp.concatenate([own_keys, own_keys[block_numbers]], axis=1)
        far_values = jnp.concatenate([own_values, own_values[block_numbers]], axis=1)
        far_scores = jnp.einsum('nqhd,nkhd->nhqk', far_queries, far_keys, precision=highest) * score_scale
        far_weights = soft_weights(far_scores, None)
        far_out = jnp.einsum('nhqk,nkhd->nqhd', far_weights.astype(jnp.float32), far_values, precision=highest).reshape(SEQ, dilated_width)
        heads_out = jnp.concatenate([near_out, far_out], axis=1).astype(jnp.bfloat16)
        updated = (hidden_f + jnp.dot(heads_out, weight_out, preferred_element_type=jnp.float32)).astype(jnp.bfloat16)
        term = lax.optimization_barrier(jnp.sum(norm_rows(updated.astype(jnp.float32)) * read_vector, axis=1))
        return (updated, term)
    results = []
    for micro_index in range(MICRO):
        start_input = series[order[micro_index]]
        final_state, layer_terms = lax.scan(layer_step, start_input, (query_key_value_weight, output_weight, gain, readout_weight))
        results.append(lax.optimization_barrier(jnp.sum(layer_terms, axis=0)))
    totals = jnp.stack(results)
    return totals.reshape(MICRO, TILES, ROWS)
```

```python
import functools

import jax
import jax.numpy as jnp
from jax import lax
from jax.experimental import pallas as pl
from jax.experimental.pallas import tpu as pltpu
from jax.sharding import PartitionSpec as P

HEADS = 4
HD = 64
BLK = 64
EPSILON = 1e-05
LAYERS = 16
MICRO = 7
ROWS = 128
D = 1024
NEAR = HEADS * HD
SLOTS = 8
AHEAD = 3
Z = 16
MESH = pl.DeviceIdType.MESH
BF = jnp.bfloat16
F32 = jnp.float32
NEG = -1e30


def compute_section(b):
    y = b // 2
    return 4 * y + 2 * (b % 2) + y % 2


def relay_section(w):
    y = w // 2
    return 4 * y + 2 * (w % 2) + 1 - y % 2


def colour(section):
    x, y = section % 4, section // 4
    return 2 * (y % 2) + (x // 2 + y // 2) % 2


def landed(ref, sem):
    pltpu.make_async_copy(ref, ref, sem).wait()


def dot(a, b):
    return jnp.dot(a, b, preferred_element_type=F32)


def scores_of(q, k):
    return lax.dot_general(q, k, (((1,), (1,)), ((), ())), preferred_element_type=F32)


def attend(q, parts):
    scores = []
    for keys, _, mask in parts:
        s = scores_of(q, keys)
        scores.append(s if mask is None else jnp.where(mask, s, NEG))
    top = functools.reduce(jnp.maximum, scores)
    top = jnp.max(top, axis=-1, keepdims=True)
    raised = [jnp.exp(s - top) for s in scores]
    total = jnp.sum(functools.reduce(jnp.add, raised), axis=-1, keepdims=True)
    out = functools.reduce(
        jnp.add, [dot(p.astype(BF), v) for p, (_, v, _) in zip(raised, parts)]
    )
    return (out / total).astype(BF)


def kernel(
    series, wqkv, wout, gain, readv, dil, order, out,
    stage, ser_rx, h, grs, wq, wo, relay_q, relay_o, near_rx, far_rx, near_own, far_own, qs, heads, totals, out_rx,
    ser_send, ser_recv, gr_send, gr_recv, root_send, relay_recv, rl_send, w_recv, fw_send, fw_recv,
    near_send, near_recv, far_send, far_recv, out_send, out_recv, credit,
):
    sec = lax.axis_index("section")
    tm = lax.axis_index("tm")
    x, y = sec % 4, sec // 4
    z, c = tm // 2, tm % 2
    is_compute = (x + y) % 2 == 0
    micro = 2 * y + x // 2
    shard = Z * c + z
    sibling = (sec, 2 * z + 1 - c)
    neighbours = (
        4 * y + (x + 1) % 4,
        4 * y + (x + 3) % 4,
        4 * ((y + 1) % 4) + x,
        4 * ((y + 3) % 4) + x,
    )

    def copy(src, dst, send, recv, device):
        return pltpu.make_async_remote_copy(
            src_ref=src, dst_ref=dst, send_sem=send, recv_sem=recv, device_id=device, device_id_type=MESH
        )

    def send_or_keep(src, dst, send, recv, device):
        here = (device[0] == sec) & (device[1] == tm)

        @pl.when(here)
        def _():
            pltpu.make_async_copy(src, dst, recv).start()

        @pl.when(jnp.logical_not(here))
        def _():
            copy(src, dst, send, recv, device).start()

    def sent_unless_kept(src, dst, send, recv, device):
        here = (device[0] == sec) & (device[1] == tm)

        @pl.when(jnp.logical_not(here))
        def _():
            copy(src, dst, send, recv, device).wait_send()

    home = 2 * (tm % Z) + tm // Z

    def series_copy(b):
        m = jnp.minimum(b, MICRO - 1)
        return (stage.at[m], ser_rx.at[sec], ser_send.at[b], ser_recv.at[sec], (compute_section(b), home))

    def gain_copy(b):
        return (gain, grs.at[sec, 0], gr_send.at[b, 0], gr_recv.at[sec, 0], (compute_section(b), tm))

    def readv_copy(b):
        return (readv, grs.at[sec, 1], gr_send.at[b, 1], gr_recv.at[sec, 1], (compute_section(b), tm))

    def root_copies(w):
        to = relay_section(w)
        e = 4 * c + colour(to)
        device = (to, tm)
        return (
            (wqkv.at[0, pl.ds(pl.multiple_of(e * 128, 128), 128)], relay_q.at[sec], root_send.at[w, 0], relay_recv.at[sec, 0], device),
            (wout.at[0, pl.ds(pl.multiple_of(e * 64, 64), 64)], relay_o.at[sec], root_send.at[w, 1], relay_recv.at[sec, 1], device),
        )

    def root_start():
        @pl.loop(0, 8)
        def _(w):
            for args in root_copies(w):
                send_or_keep(*args)

    first_step = jnp.maximum(sec - AHEAD, 0)

    for m in range(MICRO):
        slot_of = jnp.full((ROWS, 64), order[m], jnp.int32)
        picked = series[0].astype(F32)
        for k in range(1, MICRO):
            picked = jnp.where(slot_of == k, series[k].astype(F32), picked)
        stage[m] = picked.astype(BF)

    @pl.when(first_step == 0)
    def _():
        root_start()

    @pl.loop(0, 8)
    def _(b):
        send_or_keep(*series_copy(b))
        send_or_keep(*gain_copy(b))
        send_or_keep(*readv_copy(b))

    mine = colour(sec)
    eighth = 4 * c + mine

    def relay_copies(step, j):
        slot = step % SLOTS
        device = (neighbours[j], tm)
        return (
            copy(relay_q.at[step], wq.at[slot, pl.ds(pl.multiple_of(eighth * 128, 128), 128)], rl_send.at[step, j, 0], w_recv.at[slot, mine, 0], device),
            copy(relay_o.at[step], wo.at[slot, pl.ds(pl.multiple_of(eighth * 64, 64), 64)], rl_send.at[step, j, 1], w_recv.at[slot, mine, 1], device),
        )

    @pl.when(jnp.logical_not(is_compute))
    def _():
        @pl.loop(0, LAYERS)
        def _(step):
            @pl.when((step == first_step) & (step > 0))
            def _():
                root_start()

            @pl.when(step >= SLOTS)
            def _():
                for j in range(4):
                    pl.semaphore_wait(credit.at[j], 1)

            landed(relay_q.at[step], relay_recv.at[step, 0])
            for j in range(4):
                relay_copies(step, j)[0].start()
            landed(relay_o.at[step], relay_recv.at[step, 1])
            for j in range(4):
                relay_copies(step, j)[1].start()

        @pl.loop(0, LAYERS)
        def _(step):
            for j in range(4):
                for one in relay_copies(step, j):
                    one.wait_send()

    def half_copies(step):
        slot = step % SLOTS
        half_q = wq.at[slot, pl.ds(pl.multiple_of(c * 512, 512), 512)]
        half_o = wo.at[slot, pl.ds(pl.multiple_of(c * 256, 256), 256)]
        return (
            copy(half_q, half_q, fw_send.at[slot, 0], fw_recv.at[slot, 0], sibling),
            copy(half_o, half_o, fw_send.at[slot, 1], fw_recv.at[slot, 1], sibling),
        )

    def landed_half(step, part):
        slot = step % SLOTS
        landed((wq.at[slot, pl.ds(0, 512)], wo.at[slot, pl.ds(0, 256)])[part], fw_recv.at[slot, part])

    def share_half(step):
        slot = step % SLOTS
        for q in range(4):
            e = 4 * c + q
            landed(wq.at[slot, pl.ds(pl.multiple_of(e * 128, 128), 128)], w_recv.at[slot, q, 0])
        half_copies(step)[0].start()
        for q in range(4):
            e = 4 * c + q
            landed(wo.at[slot, pl.ds(pl.multiple_of(e * 64, 64), 64)], w_recv.at[slot, q, 1])
        half_copies(step)[1].start()

    def near_copy(step, distance):
        other = (shard + distance) % (2 * Z)
        device = (sec, 2 * (other % Z) + other // Z)
        return copy(near_own, near_rx.at[step, distance - 1], near_send.at[distance - 1], near_recv.at[step, distance - 1], device)

    def far_copy(step):
        return copy(far_own, far_rx.at[step], far_send.at[0], far_recv.at[step], sibling)

    def layer(step):
        slot = step % SLOTS

        @pl.when((step == first_step) & (step > 0))
        def _():
            root_start()

        landed_half(step, 0)
        landed(grs.at[step, 0], gr_recv.at[step, 0])
        hidden = h[...].astype(F32)
        scale = lax.rsqrt(jnp.mean(hidden * hidden, axis=-1, keepdims=True) + EPSILON)
        normed = (hidden * scale * grs[step, 0]).astype(BF)
        near_own[:, :NEAR] = dot(normed, wq[slot, :, 512:768]).astype(BF)
        near_own[:, NEAR:] = dot(normed, wq[slot, :, 1024:1280]).astype(BF)
        near_copy(step, 1).start()
        near_copy(step, 2).start()
        far_own[:, :NEAR] = dot(normed, wq[slot, :, 768:1024]).astype(BF)
        far_own[:, NEAR:] = dot(normed, wq[slot, :, 1280:1536]).astype(BF)
        far_copy(step).start()
        qs[...] = (dot(normed, wq[slot, :, :512]) * (HD**-0.5)).astype(BF)

        row = lax.broadcasted_iota(jnp.int32, (ROWS, ROWS), 0)
        col = lax.broadcasted_iota(jnp.int32, (ROWS, ROWS), 1)
        same = (row < BLK) == (col < BLK)
        far_copy(step).wait_recv()
        block = jnp.where(row < BLK, dil[2 * shard], dil[2 * shard + 1])
        wanted = jnp.where(col < BLK, 0, 1) == block
        for head in range(HEADS):
            k = slice(head * HD, (head + 1) * HD)
            v = slice(NEAR + head * HD, NEAR + (head + 1) * HD)
            q = qs[:, NEAR + head * HD : NEAR + (head + 1) * HD]
            heads[:, NEAR + head * HD : NEAR + (head + 1) * HD] = attend(
                q,
                (
                    (far_own[:, k], far_own[:, v], same),
                    (far_rx[step, :, k], far_rx[step, :, v], wanted),
                ),
            )

        @pl.when(step + 1 < LAYERS)
        def _():
            share_half(step + 1)

        near_copy(step, 1).wait_recv()
        near_copy(step, 2).wait_recv()
        oldest = (col > row) & (shard >= 2)
        middle = (col >= 0) & (shard >= 1)
        for head in range(HEADS):
            k = slice(head * HD, (head + 1) * HD)
            v = slice(NEAR + head * HD, NEAR + (head + 1) * HD)
            heads[:, k] = attend(
                qs[:, k],
                (
                    (near_own[:, k], near_own[:, v], col <= row),
                    (near_rx[step, 0, :, k], near_rx[step, 0, :, v], middle),
                    (near_rx[step, 1, :, k], near_rx[step, 1, :, v], oldest),
                ),
            )
        landed_half(step, 1)
        landed(grs.at[step, 1], gr_recv.at[step, 1])
        updated = (h[...].astype(F32) + dot(heads[...], wo[slot])).astype(BF)
        h[...] = updated
        u = updated.astype(F32)
        scale = lax.rsqrt(jnp.mean(u * u, axis=-1, keepdims=True) + EPSILON)
        term = jnp.sum(u * scale * grs[step, 1], axis=-1, keepdims=True)
        totals[...] += jnp.broadcast_to(term, (ROWS, 128))

        near_copy(step, 1).wait_send()
        near_copy(step, 2).wait_send()
        far_copy(step).wait_send()
        for one in half_copies(step):
            one.wait_send()

        @pl.when(step + SLOTS < LAYERS)
        def _():
            for j in range(4):
                pl.semaphore_signal(credit.at[j ^ 1], inc=1, device_id=(neighbours[j], tm), device_id_type=MESH)

    def result_copy(s):
        return (totals.at[pl.ds(pl.multiple_of(8 * s, 8), 8)], out_rx.at[micro], out_send.at[s], out_recv.at[micro], (s, shard))

    @pl.when(is_compute)
    def _():
        totals[...] = jnp.zeros_like(totals)
        for s in range(LAYERS):
            landed(ser_rx.at[s], ser_recv.at[s])
            h[:, s * 64 : (s + 1) * 64] = ser_rx[s]
        share_half(0)

        @pl.loop(0, LAYERS)
        def _(step):
            layer(step)

        @pl.when(micro < MICRO)
        def _():
            @pl.loop(0, LAYERS)
            def _(s):
                send_or_keep(*result_copy(s))

    lane = lax.broadcasted_iota(jnp.int32, (8, 128), 1)
    line = lax.broadcasted_iota(jnp.int32, (8, 128), 0)
    for m in range(MICRO):
        landed(out_rx.at[m], out_recv.at[m])
        turned = jnp.sum(jnp.where(lane == line, out_rx[m], 0.0), axis=0, keepdims=True)
        out[m] = turned[:, :8]

    @pl.when(is_compute & (micro < MICRO))
    def _():
        @pl.loop(0, LAYERS)
        def _(s):
            sent_unless_kept(*result_copy(s))

    @pl.loop(0, 8)
    def _(b):
        sent_unless_kept(*series_copy(b))
        sent_unless_kept(*gain_copy(b))
        sent_unless_kept(*readv_copy(b))
        for args in root_copies(b):
            sent_unless_kept(*args)


def local(series, query_key_value_weight, output_weight, gain, readout_weight, dilation_block, order):
    dma = pltpu.SemaphoreType.DMA
    vmem = pl.BlockSpec(memory_space=pltpu.VMEM)
    hbm = pl.BlockSpec(memory_space=pl.ANY)
    smem = pl.BlockSpec(memory_space=pltpu.SMEM)
    return pl.pallas_call(
        kernel,
        out_shape=jax.ShapeDtypeStruct((MICRO, 1, 8), F32),
        in_specs=[vmem, hbm, hbm, vmem, vmem, smem, smem],
        out_specs=vmem,
        scratch_shapes=[
            pltpu.VMEM((MICRO, ROWS, 64), BF),
            pltpu.VMEM((LAYERS, ROWS, 64), BF),
            pltpu.VMEM((ROWS, D), BF),
            pltpu.VMEM((LAYERS, 2, 1, D), F32),
            pltpu.VMEM((SLOTS, D, 1536), BF),
            pltpu.VMEM((SLOTS, 512, D), BF),
            pltpu.VMEM((LAYERS, 128, 1536), BF),
            pltpu.VMEM((LAYERS, 64, D), BF),
            pltpu.VMEM((LAYERS, 2, ROWS, 2 * NEAR), BF),
            pltpu.VMEM((LAYERS, ROWS, 2 * NEAR), BF),
            pltpu.VMEM((ROWS, 2 * NEAR), BF),
            pltpu.VMEM((ROWS, 2 * NEAR), BF),
            pltpu.VMEM((ROWS, 512), BF),
            pltpu.VMEM((ROWS, 512), BF),
            pltpu.VMEM((ROWS, 128), F32),
            pltpu.VMEM((MICRO, 8, 128), F32),
            dma((8,)), dma((LAYERS,)),
            dma((8, 2)), dma((LAYERS, 2)),
            dma((8, 2)), dma((LAYERS, 2)),
            dma((LAYERS, 4, 2)), dma((SLOTS, 4, 2)),
            dma((SLOTS, 2)), dma((SLOTS, 2)),
            dma((2,)), dma((LAYERS, 2)),
            dma((1,)), dma((LAYERS,)),
            dma((LAYERS,)), dma((MICRO,)),
            pltpu.SemaphoreType.REGULAR((4,)),
        ],
        compiler_params=pltpu.CompilerParams(has_side_effects=True, vmem_limit_bytes=58 * 2**20),
    )(series, query_key_value_weight, output_weight, gain, readout_weight, dilation_block, order)


def solution(mesh):
    placed = (
        P(None, "tm", "section"),
        P("section", None, None),
        P("section", None, None),
        P("section", None),
        P("section", None),
        P(),
        P(),
    )
    return jax.shard_map(
        local, mesh=mesh, in_specs=placed, out_specs=P(None, "tm", "section"), check_vma=False
    )
```

```python
import functools

import jax
import jax.numpy as jnp
from jax import lax
from jax.experimental import pallas as pl
from jax.experimental.pallas import tpu as pltpu
from jax.sharding import PartitionSpec as P

HEADS = 4
HD = 64
BLK = 64
EPSILON = 1e-05
LAYERS = 16
MICRO = 7
ROWS = 128
D = 1024
NEAR = HEADS * HD
SLOTS = 8
AHEAD = 4
Z = 16
MESH = pl.DeviceIdType.MESH
BF = jnp.bfloat16
F32 = jnp.float32
NEG = -1e30


def compute_section(b):
    y = b // 2
    return 4 * y + 2 * (b % 2) + y % 2


def relay_section(w):
    y = w // 2
    return 4 * y + 2 * (w % 2) + 1 - y % 2


def colour(section):
    x, y = section % 4, section // 4
    return 2 * (y % 2) + (x // 2 + y // 2) % 2


def landed(ref, sem):
    pltpu.make_async_copy(ref, ref, sem).wait()


def dot(a, b):
    return jnp.dot(a, b, preferred_element_type=F32)


def scores_of(q, k):
    return lax.dot_general(q, k, (((1,), (1,)), ((), ())), preferred_element_type=F32)


def attend(q, parts):
    scores = []
    for keys, _, mask in parts:
        s = scores_of(q, keys)
        scores.append(s if mask is None else jnp.where(mask, s, NEG))
    top = functools.reduce(jnp.maximum, scores)
    top = jnp.max(top, axis=-1, keepdims=True)
    raised = [jnp.exp(s - top) for s in scores]
    total = jnp.sum(functools.reduce(jnp.add, raised), axis=-1, keepdims=True)
    out = functools.reduce(
        jnp.add, [dot(p.astype(BF), v) for p, (_, v, _) in zip(raised, parts)]
    )
    return (out / total).astype(BF)


def kernel(
    series, wqkv, wout, gain, readv, dil, order, out,
    stage, ser_rx, h, grs, wq, wo, relay_q, relay_o, near_rx, far_rx, near_own, far_own, qs, heads, totals, out_rx,
    ser_send, ser_recv, gr_send, gr_recv, root_send, relay_recv, swap_send, rl_send, w_recv, fw_send, fw_recv,
    near_send, near_recv, far_send, far_recv, out_send, out_recv, credit,
):
    sec = lax.axis_index("section")
    tm = lax.axis_index("tm")
    x, y = sec % 4, sec // 4
    z, c = tm // 2, tm % 2
    is_compute = (x + y) % 2 == 0
    micro = 2 * y + x // 2
    shard = Z * c + z
    sibling = (sec, 2 * z + 1 - c)
    neighbours = (
        4 * y + (x + 1) % 4,
        4 * y + (x + 3) % 4,
        4 * ((y + 1) % 4) + x,
        4 * ((y + 3) % 4) + x,
    )

    def copy(src, dst, send, recv, device):
        return pltpu.make_async_remote_copy(
            src_ref=src, dst_ref=dst, send_sem=send, recv_sem=recv, device_id=device, device_id_type=MESH
        )

    def send_or_keep(src, dst, send, recv, device):
        here = (device[0] == sec) & (device[1] == tm)

        @pl.when(here)
        def _():
            pltpu.make_async_copy(src, dst, recv).start()

        @pl.when(jnp.logical_not(here))
        def _():
            copy(src, dst, send, recv, device).start()

    def sent_unless_kept(src, dst, send, recv, device):
        here = (device[0] == sec) & (device[1] == tm)

        @pl.when(jnp.logical_not(here))
        def _():
            copy(src, dst, send, recv, device).wait_send()

    home = 2 * (tm % Z) + tm // Z

    def series_copy(b):
        m = jnp.minimum(b, MICRO - 1)
        return (stage.at[m], ser_rx.at[sec], ser_send.at[b], ser_recv.at[sec], (compute_section(b), home))

    def gain_copy(b):
        return (gain, grs.at[sec, 0], gr_send.at[b, 0], gr_recv.at[sec, 0], (compute_section(b), tm))

    def readv_copy(b):
        return (readv, grs.at[sec, 1], gr_send.at[b, 1], gr_recv.at[sec, 1], (compute_section(b), tm))

    part = z % 4

    def part_q(step, k):
        return relay_q.at[step, pl.ds(pl.multiple_of(k * 32, 32), 32)]

    def part_o(step, k):
        return relay_o.at[step, pl.ds(pl.multiple_of(k * 16, 16), 16)]

    def part_copies(step, i):
        to = (z + (1, Z - 1, Z + 2 - 4 * c)[i]) % Z
        device = (sec, 2 * to + c)
        return (
            copy(part_q(step, part), part_q(step, part), swap_send.at[step, i, 0], relay_recv.at[step, part, 0], device),
            copy(part_o(step, part), part_o(step, part), swap_send.at[step, i, 1], relay_recv.at[step, part, 1], device),
        )

    def swap_parts(step):
        landed(part_q(step, part), relay_recv.at[step, part, 0])
        landed(part_o(step, part), relay_recv.at[step, part, 1])
        for i in range(3):
            for one in part_copies(step, i):
                one.start()

    def root_copies(w):
        to = relay_section(w)
        e = 4 * c + colour(to)
        device = (to, tm)
        return (
            (wqkv.at[0, pl.ds(pl.multiple_of(e * 128 + part * 32, 32), 32)], part_q(sec, part), root_send.at[w, 0], relay_recv.at[sec, part, 0], device),
            (wout.at[0, pl.ds(pl.multiple_of(e * 64 + part * 16, 16), 16)], part_o(sec, part), root_send.at[w, 1], relay_recv.at[sec, part, 1], device),
        )

    def root_start():
        @pl.loop(0, 8)
        def _(w):
            for args in root_copies(w):
                send_or_keep(*args)

    first_step = jnp.maximum(sec - AHEAD, 0)

    for m in range(MICRO):
        slot_of = jnp.full((ROWS, 64), order[m], jnp.int32)
        picked = series[0].astype(F32)
        for k in range(1, MICRO):
            picked = jnp.where(slot_of == k, series[k].astype(F32), picked)
        stage[m] = picked.astype(BF)

    @pl.when(first_step == 0)
    def _():
        root_start()

    @pl.loop(0, 8)
    def _(b):
        send_or_keep(*series_copy(b))
        send_or_keep(*gain_copy(b))
        send_or_keep(*readv_copy(b))

    mine = colour(sec)
    eighth = 4 * c + mine

    def relay_copy_q(step, j):
        slot = step % SLOTS
        return copy(relay_q.at[step], wq.at[slot, pl.ds(pl.multiple_of(eighth * 128, 128), 128)], rl_send.at[step, j, 0], w_recv.at[slot, mine, 0], (neighbours[j], tm))

    def relay_copy_o(step, j):
        slot = step % SLOTS
        return copy(relay_o.at[step], wo.at[slot, pl.ds(pl.multiple_of(eighth * 64, 64), 64)], rl_send.at[step, j, 1], w_recv.at[slot, mine, 1], (neighbours[j], tm))

    @pl.when(jnp.logical_not(is_compute))
    def _():
        swap_parts(0)

        @pl.loop(0, LAYERS)
        def _(step):
            @pl.when((step == first_step) & (step > 0))
            def _():
                root_start()

            @pl.when(step >= SLOTS)
            def _():
                for j in range(4):
                    pl.semaphore_wait(credit.at[j], 1)

            for d in range(1, 4):
                k = (part + d) % 4
                landed(part_q(step, k), relay_recv.at[step, k, 0])
                landed(part_o(step, k), relay_recv.at[step, k, 1])
            for j in range(4):
                relay_copy_q(step, j).start()
            for j in range(4):
                relay_copy_o(step, j).start()

            @pl.when(step + 1 < LAYERS)
            def _():
                swap_parts(step + 1)

        @pl.loop(0, LAYERS)
        def _(step):
            for j in range(4):
                relay_copy_q(step, j).wait_send()
                relay_copy_o(step, j).wait_send()
            for i in range(3):
                for one in part_copies(step, i):
                    one.wait_send()

    def half_copy_q(step):
        slot = step % SLOTS
        half = wq.at[slot, pl.ds(pl.multiple_of(c * 512, 512), 512)]
        return copy(half, half, fw_send.at[slot, 0], fw_recv.at[slot, 0], sibling)

    def half_copy_o(step):
        slot = step % SLOTS
        half = wo.at[slot, pl.ds(pl.multiple_of(c * 256, 256), 256)]
        return copy(half, half, fw_send.at[slot, 1], fw_recv.at[slot, 1], sibling)

    def landed_half(step, which):
        slot = step % SLOTS
        landed((wq.at[slot, pl.ds(0, 512)], wo.at[slot, pl.ds(0, 256)])[which], fw_recv.at[slot, which])

    def share_half(step):
        slot = step % SLOTS
        for q in range(4):
            e = 4 * c + q
            landed(wq.at[slot, pl.ds(pl.multiple_of(e * 128, 128), 128)], w_recv.at[slot, q, 0])
        half_copy_q(step).start()
        for q in range(4):
            e = 4 * c + q
            landed(wo.at[slot, pl.ds(pl.multiple_of(e * 64, 64), 64)], w_recv.at[slot, q, 1])
        half_copy_o(step).start()

    def near_copy(step, distance):
        other = (shard + distance) % (2 * Z)
        device = (sec, 2 * (other % Z) + other // Z)
        return copy(near_own, near_rx.at[step, distance - 1], near_send.at[distance - 1], near_recv.at[step, distance - 1], device)

    def far_copy(step):
        return copy(far_own, far_rx.at[step], far_send.at[0], far_recv.at[step], sibling)

    def layer(step):
        slot = step % SLOTS

        @pl.when((step == first_step) & (step > 0))
        def _():
            root_start()

        landed_half(step, 0)
        landed(grs.at[step, 0], gr_recv.at[step, 0])
        hidden = h[...].astype(F32)
        scale = lax.rsqrt(jnp.mean(hidden * hidden, axis=-1, keepdims=True) + EPSILON)
        normed = (hidden * scale * grs[step, 0]).astype(BF)
        near_own[:, :NEAR] = dot(normed, wq[slot, :, 512:768]).astype(BF)
        near_own[:, NEAR:] = dot(normed, wq[slot, :, 1024:1280]).astype(BF)
        near_copy(step, 1).start()
        near_copy(step, 2).start()
        far_own[:, :NEAR] = dot(normed, wq[slot, :, 768:1024]).astype(BF)
        far_own[:, NEAR:] = dot(normed, wq[slot, :, 1280:1536]).astype(BF)
        far_copy(step).start()
        qs[...] = (dot(normed, wq[slot, :, :512]) * (HD**-0.5)).astype(BF)

        row = lax.broadcasted_iota(jnp.int32, (ROWS, ROWS), 0)
        col = lax.broadcasted_iota(jnp.int32, (ROWS, ROWS), 1)
        same = (row < BLK) == (col < BLK)
        far_copy(step).wait_recv()
        block = jnp.where(row < BLK, dil[2 * shard], dil[2 * shard + 1])
        wanted = jnp.where(col < BLK, 0, 1) == block
        for head in range(HEADS):
            k = slice(head * HD, (head + 1) * HD)
            v = slice(NEAR + head * HD, NEAR + (head + 1) * HD)
            q = qs[:, NEAR + head * HD : NEAR + (head + 1) * HD]
            heads[:, NEAR + head * HD : NEAR + (head + 1) * HD] = attend(
                q,
                (
                    (far_own[:, k], far_own[:, v], same),
                    (far_rx[step, :, k], far_rx[step, :, v], wanted),
                ),
            )

        @pl.when(step + 1 < LAYERS)
        def _():
            share_half(step + 1)

        near_copy(step, 1).wait_recv()
        near_copy(step, 2).wait_recv()
        oldest = (col > row) & (shard >= 2)
        middle = (col >= 0) & (shard >= 1)
        for head in range(HEADS):
            k = slice(head * HD, (head + 1) * HD)
            v = slice(NEAR + head * HD, NEAR + (head + 1) * HD)
            heads[:, k] = attend(
                qs[:, k],
                (
                    (near_own[:, k], near_own[:, v], col <= row),
                    (near_rx[step, 0, :, k], near_rx[step, 0, :, v], middle),
                    (near_rx[step, 1, :, k], near_rx[step, 1, :, v], oldest),
                ),
            )
        landed_half(step, 1)
        landed(grs.at[step, 1], gr_recv.at[step, 1])
        updated = (h[...].astype(F32) + dot(heads[...], wo[slot])).astype(BF)
        h[...] = updated
        u = updated.astype(F32)
        scale = lax.rsqrt(jnp.mean(u * u, axis=-1, keepdims=True) + EPSILON)
        term = jnp.sum(u * scale * grs[step, 1], axis=-1, keepdims=True)
        totals[...] += jnp.broadcast_to(term, (ROWS, 128))

        near_copy(step, 1).wait_send()
        near_copy(step, 2).wait_send()
        far_copy(step).wait_send()
        half_copy_q(step).wait_send()
        half_copy_o(step).wait_send()

        @pl.when(step + SLOTS < LAYERS)
        def _():
            for j in range(4):
                pl.semaphore_signal(credit.at[j ^ 1], inc=1, device_id=(neighbours[j], tm), device_id_type=MESH)

    def result_copy(s):
        return (totals.at[pl.ds(pl.multiple_of(8 * s, 8), 8)], out_rx.at[micro], out_send.at[s], out_recv.at[micro], (s, shard))

    @pl.when(is_compute)
    def _():
        totals[...] = jnp.zeros_like(totals)
        for s in range(LAYERS):
            landed(ser_rx.at[s], ser_recv.at[s])
            h[:, s * 64 : (s + 1) * 64] = ser_rx[s]
        share_half(0)

        @pl.loop(0, LAYERS)
        def _(step):
            layer(step)

        @pl.when(micro < MICRO)
        def _():
            @pl.loop(0, LAYERS)
            def _(s):
                send_or_keep(*result_copy(s))

    lane = lax.broadcasted_iota(jnp.int32, (8, 128), 1)
    line = lax.broadcasted_iota(jnp.int32, (8, 128), 0)
    for m in range(MICRO):
        landed(out_rx.at[m], out_recv.at[m])
        turned = jnp.sum(jnp.where(lane == line, out_rx[m], 0.0), axis=0, keepdims=True)
        out[m] = turned[:, :8]

    @pl.when(is_compute & (micro < MICRO))
    def _():
        @pl.loop(0, LAYERS)
        def _(s):
            sent_unless_kept(*result_copy(s))

    @pl.loop(0, 8)
    def _(b):
        sent_unless_kept(*series_copy(b))
        sent_unless_kept(*gain_copy(b))
        sent_unless_kept(*readv_copy(b))
        for args in root_copies(b):
            sent_unless_kept(*args)


def local(series, query_key_value_weight, output_weight, gain, readout_weight, dilation_block, order):
    dma = pltpu.SemaphoreType.DMA
    vmem = pl.BlockSpec(memory_space=pltpu.VMEM)
    hbm = pl.BlockSpec(memory_space=pl.ANY)
    smem = pl.BlockSpec(memory_space=pltpu.SMEM)
    return pl.pallas_call(
        kernel,
        out_shape=jax.ShapeDtypeStruct((MICRO, 1, 8), F32),
        in_specs=[vmem, hbm, hbm, vmem, vmem, smem, smem],
        out_specs=vmem,
        scratch_shapes=[
            pltpu.VMEM((MICRO, ROWS, 64), BF),
            pltpu.VMEM((LAYERS, ROWS, 64), BF),
            pltpu.VMEM((ROWS, D), BF),
            pltpu.VMEM((LAYERS, 2, 1, D), F32),
            pltpu.VMEM((SLOTS, D, 1536), BF),
            pltpu.VMEM((SLOTS, 512, D), BF),
            pltpu.VMEM((LAYERS, 128, 1536), BF),
            pltpu.VMEM((LAYERS, 64, D), BF),
            pltpu.VMEM((LAYERS, 2, ROWS, 2 * NEAR), BF),
            pltpu.VMEM((LAYERS, ROWS, 2 * NEAR), BF),
            pltpu.VMEM((ROWS, 2 * NEAR), BF),
            pltpu.VMEM((ROWS, 2 * NEAR), BF),
            pltpu.VMEM((ROWS, 512), BF),
            pltpu.VMEM((ROWS, 512), BF),
            pltpu.VMEM((ROWS, 128), F32),
            pltpu.VMEM((MICRO, 8, 128), F32),
            dma((8,)), dma((LAYERS,)),
            dma((8, 2)), dma((LAYERS, 2)),
            dma((8, 2)), dma((LAYERS, 4, 2)), dma((LAYERS, 3, 2)),
            dma((LAYERS, 4, 2)), dma((SLOTS, 4, 2)),
            dma((SLOTS, 2)), dma((SLOTS, 2)),
            dma((2,)), dma((LAYERS, 2)),
            dma((1,)), dma((LAYERS,)),
            dma((LAYERS,)), dma((MICRO,)),
            pltpu.SemaphoreType.REGULAR((4,)),
        ],
        compiler_params=pltpu.CompilerParams(has_side_effects=True, vmem_limit_bytes=58 * 2**20),
    )(series, query_key_value_weight, output_weight, gain, readout_weight, dilation_block, order)


def solution(mesh):
    placed = (
        P(None, "tm", "section"),
        P("section", None, None),
        P("section", None, None),
        P("section", None),
        P("section", None),
        P(),
        P(),
    )
    return jax.shard_map(
        local, mesh=mesh, in_specs=placed, out_specs=P(None, "tm", "section"), check_vma=False
    )
```

```python
import functools

import jax
import jax.numpy as jnp
from jax import lax
from jax.experimental import pallas as pl
from jax.experimental.pallas import tpu as pltpu
from jax.sharding import PartitionSpec as P

HEADS = 4
HD = 64
BLK = 64
EPSILON = 1e-05
LAYERS = 16
MICRO = 7
ROWS = 128
D = 1024
NEAR = HEADS * HD
SLOTS = 8
AHEAD = 4
Z = 16
GREET_COMPUTE = 15 + 16 + 8 + 3
GREET_RELAY = 15 + 8 + 4
MESH = pl.DeviceIdType.MESH
BF = jnp.bfloat16
F32 = jnp.float32
NEG = -1e30


def compute_section(b):
    y = b // 2
    return 4 * y + 2 * (b % 2) + y % 2


def relay_section(w):
    y = w // 2
    return 4 * y + 2 * (w % 2) + 1 - y % 2


def colour(section):
    x, y = section % 4, section // 4
    return 2 * (y % 2) + (x // 2 + y // 2) % 2


def landed(ref, sem):
    pltpu.make_async_copy(ref, ref, sem).wait()


def dot(a, b):
    return jnp.dot(a, b, preferred_element_type=F32)


def scores_of(q, k):
    return lax.dot_general(q, k, (((1,), (1,)), ((), ())), preferred_element_type=F32)


def attend(q, parts, before=None):
    scores = []
    for keys, _, mask in parts:
        s = scores_of(q, keys)
        scores.append(s if mask is None else jnp.where(mask, s, NEG))
    top = jnp.max(functools.reduce(jnp.maximum, scores), axis=-1, keepdims=True)
    if before is not None:
        top = jnp.maximum(top, before[0])
    raised = [jnp.exp(s - top) for s in scores]
    total = jnp.sum(functools.reduce(jnp.add, raised), axis=-1, keepdims=True)
    out = functools.reduce(
        jnp.add, [dot(p.astype(BF), v) for p, (_, v, _) in zip(raised, parts)]
    )
    if before is not None:
        fade = jnp.exp(before[0] - top)
        total = total + before[1] * fade
        out = out + before[2] * fade
    return top, total, out


def weighted(state):
    _, total, out = state
    return (out / total).astype(BF)


def kernel(
    series, wqkv, wout, gain, readv, dil, order, out,
    stage, ser_rx, h, grs, wq, wo, relay_q, relay_o, near_rx, far_rx, near_own, far_own, qs, heads, totals, out_rx,
    ser_send, ser_recv, gr_send, gr_recv, root_send, relay_recv, swap_send, rl_send, w_recv, fw_send, fw_recv,
    near_send, near_recv, far_send, far_recv, out_send, out_recv, credit,
):
    sec = lax.axis_index("section")
    tm = lax.axis_index("tm")
    x, y = sec % 4, sec // 4
    z, c = tm // 2, tm % 2
    is_compute = (x + y) % 2 == 0
    micro = 2 * y + x // 2
    shard = Z * c + z
    sibling = (sec, 2 * z + 1 - c)
    neighbours = (
        4 * y + (x + 1) % 4,
        4 * y + (x + 3) % 4,
        4 * ((y + 1) % 4) + x,
        4 * ((y + 3) % 4) + x,
    )

    def copy(src, dst, send, recv, device):
        return pltpu.make_async_remote_copy(
            src_ref=src, dst_ref=dst, send_sem=send, recv_sem=recv, device_id=device, device_id_type=MESH
        )

    def send_or_keep(src, dst, send, recv, device):
        here = (device[0] == sec) & (device[1] == tm)

        @pl.when(here)
        def _():
            pltpu.make_async_copy(src, dst, recv).start()

        @pl.when(jnp.logical_not(here))
        def _():
            copy(src, dst, send, recv, device).start()

    def sent_unless_kept(src, dst, send, recv, device):
        here = (device[0] == sec) & (device[1] == tm)

        @pl.when(jnp.logical_not(here))
        def _():
            copy(src, dst, send, recv, device).wait_send()

    def near_device(distance):
        other = (shard + distance + 2 * Z) % (2 * Z)
        return (sec, 2 * (other % Z) + other // Z)

    def greet():
        barrier = pltpu.get_barrier_semaphore()

        def meet(device):
            here = (device[0] == sec) & (device[1] == tm)

            @pl.when(jnp.logical_not(here))
            def _():
                pl.semaphore_signal(barrier, inc=1, device_id=device, device_id_type=MESH)

        @pl.loop(0, LAYERS)
        def _(s):
            meet((s, tm))

        @pl.loop(0, 8)
        def _(b):
            meet((compute_section(b), home))

        @pl.when(is_compute)
        def _():
            @pl.loop(0, LAYERS)
            def _(s):
                meet((s, shard))

            meet(sibling)
            for distance in (-1, 1):
                meet(near_device(distance))

        @pl.when(jnp.logical_not(is_compute))
        def _():
            for far in (1, 2):
                meet((sec, 2 * ((z + far) % Z) + c))
                meet((sec, 2 * ((z + Z - far) % Z) + c))

        pl.semaphore_wait(barrier, jnp.where(is_compute, jnp.where(shard == tm, GREET_COMPUTE - 2, GREET_COMPUTE), GREET_RELAY))

    home = 2 * (tm % Z) + tm // Z

    def series_copy(b):
        m = jnp.minimum(b, MICRO - 1)
        return (stage.at[m], ser_rx.at[pl.ds(pl.multiple_of(sec * 64, 64), 64)], ser_send.at[b], ser_recv.at[sec], (compute_section(b), home))

    def gain_copy(b):
        return (gain, grs.at[sec, 0], gr_send.at[b, 0], gr_recv.at[sec, 0], (compute_section(b), tm))

    def readv_copy(b):
        return (readv, grs.at[sec, 1], gr_send.at[b, 1], gr_recv.at[sec, 1], (compute_section(b), tm))

    part = z % 4

    def part_q(step, k):
        return relay_q.at[step, pl.ds(pl.multiple_of(k * 32, 32), 32)]

    def part_o(step, k):
        return relay_o.at[step, pl.ds(pl.multiple_of(k * 16, 16), 16)]

    def part_copies(step, i):
        to = (z + (1, Z - 1, Z + 2 - 4 * c)[i]) % Z
        device = (sec, 2 * to + c)
        return (
            copy(part_q(step, part), part_q(step, part), swap_send.at[step, i, 0], relay_recv.at[step, part, 0], device),
            copy(part_o(step, part), part_o(step, part), swap_send.at[step, i, 1], relay_recv.at[step, part, 1], device),
        )

    def swap_parts(step):
        landed(part_q(step, part), relay_recv.at[step, part, 0])
        landed(part_o(step, part), relay_recv.at[step, part, 1])
        for i in range(3):
            for one in part_copies(step, i):
                one.start()

    def root_copies(w):
        to = relay_section(w)
        e = 4 * c + colour(to)
        device = (to, tm)
        return (
            (wqkv.at[0, pl.ds(pl.multiple_of(e * 128 + part * 32, 32), 32)], part_q(sec, part), root_send.at[w, 0], relay_recv.at[sec, part, 0], device),
            (wout.at[0, pl.ds(pl.multiple_of(e * 64 + part * 16, 16), 16)], part_o(sec, part), root_send.at[w, 1], relay_recv.at[sec, part, 1], device),
        )

    def root_start():
        @pl.loop(0, 8)
        def _(w):
            for args in root_copies(w):
                send_or_keep(*args)

    first_step = jnp.maximum(sec - AHEAD, 0)

    greet()

    @pl.when(first_step == 0)
    def _():
        root_start()

    for m in range(MICRO):
        slot_of = jnp.full((64, ROWS), order[m], jnp.int32)
        picked = series[0].astype(F32)
        for k in range(1, MICRO):
            picked = jnp.where(slot_of == k, series[k].astype(F32), picked)
        stage[m] = picked.astype(BF)

    @pl.loop(0, 8)
    def _(b):
        send_or_keep(*series_copy(b))
        send_or_keep(*gain_copy(b))
        send_or_keep(*readv_copy(b))

    mine = colour(sec)
    eighth = 4 * c + mine

    def relay_copy_q(step, j):
        slot = step % SLOTS
        return copy(relay_q.at[step], wq.at[slot, pl.ds(pl.multiple_of(eighth * 128, 128), 128)], rl_send.at[step, j, 0], w_recv.at[slot, mine, 0], (neighbours[j], tm))

    def relay_copy_o(step, j):
        slot = step % SLOTS
        return copy(relay_o.at[step], wo.at[slot, pl.ds(pl.multiple_of(eighth * 64, 64), 64)], rl_send.at[step, j, 1], w_recv.at[slot, mine, 1], (neighbours[j], tm))

    @pl.when(jnp.logical_not(is_compute))
    def _():
        swap_parts(0)

        @pl.loop(0, LAYERS)
        def _(step):
            @pl.when((step == first_step) & (step > 0))
            def _():
                root_start()

            @pl.when(step >= SLOTS)
            def _():
                for j in range(4):
                    pl.semaphore_wait(credit.at[j], 1)

            for d in range(1, 4):
                k = (part + d) % 4
                landed(part_q(step, k), relay_recv.at[step, k, 0])
                landed(part_o(step, k), relay_recv.at[step, k, 1])
            for j in range(4):
                relay_copy_q(step, j).start()
            for j in range(4):
                relay_copy_o(step, j).start()

            @pl.when(step + 1 < LAYERS)
            def _():
                swap_parts(step + 1)

        @pl.loop(0, LAYERS)
        def _(step):
            for j in range(4):
                relay_copy_q(step, j).wait_send()
                relay_copy_o(step, j).wait_send()
            for i in range(3):
                for one in part_copies(step, i):
                    one.wait_send()

    def half_copy_q(step):
        slot = step % SLOTS
        half = wq.at[slot, pl.ds(pl.multiple_of(c * 512, 512), 512)]
        return copy(half, half, fw_send.at[slot, 0], fw_recv.at[slot, 0], sibling)

    def half_copy_o(step):
        slot = step % SLOTS
        half = wo.at[slot, pl.ds(pl.multiple_of(c * 256, 256), 256)]
        return copy(half, half, fw_send.at[slot, 1], fw_recv.at[slot, 1], sibling)

    def landed_half(step, which):
        slot = step % SLOTS
        landed((wq.at[slot, pl.ds(0, 512)], wo.at[slot, pl.ds(0, 256)])[which], fw_recv.at[slot, which])

    def share_half(step):
        slot = step % SLOTS
        for q in range(4):
            e = 4 * c + q
            landed(wq.at[slot, pl.ds(pl.multiple_of(e * 128, 128), 128)], w_recv.at[slot, q, 0])
        half_copy_q(step).start()
        for q in range(4):
            e = 4 * c + q
            landed(wo.at[slot, pl.ds(pl.multiple_of(e * 64, 64), 64)], w_recv.at[slot, q, 1])
        half_copy_o(step).start()

    def near_copy(step, kv):
        return copy(near_own.at[kv], near_rx.at[step, 0, kv], near_send.at[0, kv], near_recv.at[step, 0, kv], near_device(1))

    def near_pass(step, kv):
        return copy(near_rx.at[step, 0, kv], near_rx.at[step, 1, kv], near_send.at[1, kv], near_recv.at[step, 1, kv], near_device(1))

    def far_copy(step):
        return copy(far_own, far_rx.at[step], far_send.at[0], far_recv.at[step], sibling)

    def layer(step):
        slot = step % SLOTS

        @pl.when((step == first_step) & (step > 0))
        def _():
            root_start()

        landed_half(step, 0)
        landed(grs.at[step, 0], gr_recv.at[step, 0])
        hidden = h[...].astype(F32)
        scale = lax.rsqrt(jnp.mean(hidden * hidden, axis=-1, keepdims=True) + EPSILON)
        normed = (hidden * scale * grs[step, 0]).astype(BF)
        near_own[0] = dot(normed, wq[slot, :, 512:768]).astype(BF)
        near_copy(step, 0).start()
        near_own[1] = dot(normed, wq[slot, :, 1024:1280]).astype(BF)
        near_copy(step, 1).start()
        far_own[:, :NEAR] = dot(normed, wq[slot, :, 768:1024]).astype(BF)
        far_own[:, NEAR:] = dot(normed, wq[slot, :, 1280:1536]).astype(BF)
        far_copy(step).start()
        qs[...] = (dot(normed, wq[slot, :, :512]) * (HD**-0.5)).astype(BF)

        row = lax.broadcasted_iota(jnp.int32, (ROWS, ROWS), 0)
        col = lax.broadcasted_iota(jnp.int32, (ROWS, ROWS), 1)
        same = (row < BLK) == (col < BLK)
        far_copy(step).wait_recv()
        block = jnp.where(row < BLK, dil[2 * shard], dil[2 * shard + 1])
        wanted = jnp.where(col < BLK, 0, 1) == block
        for head in range(HEADS):
            k = slice(head * HD, (head + 1) * HD)
            v = slice(NEAR + head * HD, NEAR + (head + 1) * HD)
            q = qs[:, NEAR + head * HD : NEAR + (head + 1) * HD]
            heads[:, NEAR + head * HD : NEAR + (head + 1) * HD] = weighted(
                attend(
                    q,
                    (
                        (far_own[:, k], far_own[:, v], same),
                        (far_rx[step, :, k], far_rx[step, :, v], wanted),
                    ),
                )
            )
        for kv in range(2):
            near_copy(step, kv).wait_recv()
            near_pass(step, kv).start()

        @pl.when(step + 1 < LAYERS)
        def _():
            share_half(step + 1)

        oldest = (col > row) & (shard >= 2)
        middle = (col >= 0) & (shard >= 1)
        begun = []
        for head in range(HEADS):
            k = slice(head * HD, (head + 1) * HD)
            begun.append(
                attend(
                    qs[:, k],
                    (
                        (near_own[0, :, k], near_own[1, :, k], col <= row),
                        (near_rx[step, 0, 0, :, k], near_rx[step, 0, 1, :, k], middle),
                    ),
                )
            )
        for kv in range(2):
            near_pass(step, kv).wait_recv()
        for head in range(HEADS):
            k = slice(head * HD, (head + 1) * HD)
            last = (near_rx[step, 1, 0, :, k], near_rx[step, 1, 1, :, k], oldest)
            heads[:, k] = weighted(attend(qs[:, k], (last,), begun[head]))
        landed_half(step, 1)
        landed(grs.at[step, 1], gr_recv.at[step, 1])
        updated = (h[...].astype(F32) + dot(heads[...], wo[slot])).astype(BF)
        h[...] = updated
        u = updated.astype(F32)
        scale = lax.rsqrt(jnp.mean(u * u, axis=-1, keepdims=True) + EPSILON)
        term = jnp.sum(u * scale * grs[step, 1], axis=-1, keepdims=True)
        totals[...] += jnp.broadcast_to(term, (ROWS, 128))

        for kv in range(2):
            near_copy(step, kv).wait_send()
            near_pass(step, kv).wait_send()
        far_copy(step).wait_send()
        half_copy_q(step).wait_send()
        half_copy_o(step).wait_send()

        @pl.when(step + SLOTS < LAYERS)
        def _():
            for j in range(4):
                pl.semaphore_signal(credit.at[j ^ 1], inc=1, device_id=(neighbours[j], tm), device_id_type=MESH)

    def result_copy(s):
        return (totals.at[pl.ds(pl.multiple_of(8 * s, 8), 8)], out_rx.at[micro], out_send.at[s], out_recv.at[micro], (s, shard))

    @pl.when(is_compute)
    def _():
        totals[...] = jnp.zeros_like(totals)
        for s in range(LAYERS):
            landed(ser_rx.at[pl.ds(s * 64, 64)], ser_recv.at[s])
        for i in range(D // 128):
            block = slice(i * 128, (i + 1) * 128)
            h[:, block] = ser_rx[block, :].astype(F32).T.astype(BF)
        share_half(0)

        @pl.loop(0, LAYERS)
        def _(step):
            layer(step)

        @pl.when(micro < MICRO)
        def _():
            @pl.loop(0, LAYERS)
            def _(s):
                send_or_keep(*result_copy(s))

    lane = lax.broadcasted_iota(jnp.int32, (8, 128), 1)
    line = lax.broadcasted_iota(jnp.int32, (8, 128), 0)
    for m in range(MICRO):
        landed(out_rx.at[m], out_recv.at[m])
        turned = jnp.sum(jnp.where(lane == line, out_rx[m], 0.0), axis=0, keepdims=True)
        out[m] = turned[:, :8]

    @pl.when(is_compute & (micro < MICRO))
    def _():
        @pl.loop(0, LAYERS)
        def _(s):
            sent_unless_kept(*result_copy(s))

    @pl.loop(0, 8)
    def _(b):
        sent_unless_kept(*series_copy(b))
        sent_unless_kept(*gain_copy(b))
        sent_unless_kept(*readv_copy(b))
        for args in root_copies(b):
            sent_unless_kept(*args)


def local(series, query_key_value_weight, output_weight, gain, readout_weight, dilation_block, order):
    dma = pltpu.SemaphoreType.DMA
    vmem = pl.BlockSpec(memory_space=pltpu.VMEM)
    hbm = pl.BlockSpec(memory_space=pl.ANY)
    smem = pl.BlockSpec(memory_space=pltpu.SMEM)
    return pl.pallas_call(
        kernel,
        out_shape=jax.ShapeDtypeStruct((MICRO, 1, 8), F32),
        in_specs=[vmem, hbm, hbm, vmem, vmem, smem, smem],
        out_specs=vmem,
        scratch_shapes=[
            pltpu.VMEM((MICRO, 64, ROWS), BF),
            pltpu.VMEM((D, ROWS), BF),
            pltpu.VMEM((ROWS, D), BF),
            pltpu.VMEM((LAYERS, 2, 1, D), F32),
            pltpu.VMEM((SLOTS, D, 1536), BF),
            pltpu.VMEM((SLOTS, 512, D), BF),
            pltpu.VMEM((LAYERS, 128, 1536), BF),
            pltpu.VMEM((LAYERS, 64, D), BF),
            pltpu.VMEM((LAYERS, 2, 2, ROWS, NEAR), BF),
            pltpu.VMEM((LAYERS, ROWS, 2 * NEAR), BF),
            pltpu.VMEM((2, ROWS, NEAR), BF),
            pltpu.VMEM((ROWS, 2 * NEAR), BF),
            pltpu.VMEM((ROWS, 512), BF),
            pltpu.VMEM((ROWS, 512), BF),
            pltpu.VMEM((ROWS, 128), F32),
            pltpu.VMEM((MICRO, 8, 128), F32),
            dma((8,)), dma((LAYERS,)),
            dma((8, 2)), dma((LAYERS, 2)),
            dma((8, 2)), dma((LAYERS, 4, 2)), dma((LAYERS, 3, 2)),
            dma((LAYERS, 4, 2)), dma((SLOTS, 4, 2)),
            dma((SLOTS, 2)), dma((SLOTS, 2)),
            dma((2, 2)), dma((LAYERS, 2, 2)),
            dma((1,)), dma((LAYERS,)),
            dma((LAYERS,)), dma((MICRO,)),
            pltpu.SemaphoreType.REGULAR((4,)),
        ],
        compiler_params=pltpu.CompilerParams(collective_id=0, has_side_effects=True, vmem_limit_bytes=58 * 2**20),
    )(jnp.swapaxes(series, 1, 2), query_key_value_weight, output_weight, gain, readout_weight, dilation_block, order)


def solution(mesh):
    placed = (
        P(None, "tm", "section"),
        P("section", None, None),
        P("section", None, None),
        P("section", None),
        P("section", None),
        P(),
        P(),
    )
    return jax.shard_map(
        local, mesh=mesh, in_specs=placed, out_specs=P(None, "tm", "section"), check_vma=False
    )
```

```python
import functools

import jax
import jax.numpy as jnp
from jax import lax
from jax.experimental import pallas as pl
from jax.experimental.pallas import tpu as pltpu
from jax.sharding import PartitionSpec as P

HEADS = 4
HD = 64
BLK = 64
EPSILON = 1e-05
LAYERS = 16
MICRO = 7
ROWS = 128
D = 1024
NEAR = HEADS * HD
SLOTS = 8
AHEAD = 4
Z = 16
GREET_COMPUTE = 15 + 16 + 8 + 3
GREET_RELAY = 15 + 8 + 4
MESH = pl.DeviceIdType.MESH
BF = jnp.bfloat16
F32 = jnp.float32
NEG = -1e30


def compute_section(b):
    y = b // 2
    return 4 * y + 2 * (b % 2) + y % 2


def relay_section(w):
    y = w // 2
    return 4 * y + 2 * (w % 2) + 1 - y % 2


def colour(section):
    x, y = section % 4, section // 4
    return 2 * (y % 2) + (x // 2 + y // 2) % 2


def landed(ref, sem):
    pltpu.make_async_copy(ref, ref, sem).wait()


def dot(a, b):
    return jnp.dot(a, b, preferred_element_type=F32)


def scores_of(q, k):
    return lax.dot_general(q, k, (((1,), (1,)), ((), ())), preferred_element_type=F32)


def attend(q, parts, before=None):
    scores = []
    for keys, _, mask in parts:
        s = scores_of(q, keys)
        scores.append(s if mask is None else jnp.where(mask, s, NEG))
    top = jnp.max(functools.reduce(jnp.maximum, scores), axis=-1, keepdims=True)
    if before is not None:
        top = jnp.maximum(top, before[0])
    raised = [jnp.exp(s - top) for s in scores]
    total = jnp.sum(functools.reduce(jnp.add, raised), axis=-1, keepdims=True)
    out = functools.reduce(
        jnp.add, [dot(p.astype(BF), v) for p, (_, v, _) in zip(raised, parts)]
    )
    if before is not None:
        fade = jnp.exp(before[0] - top)
        total = total + before[1] * fade
        out = out + before[2] * fade
    return top, total, out


def weighted(state):
    _, total, out = state
    return (out / total).astype(BF)


def kernel(
    series, wqkv, wout, gain, readv, dil, order, out,
    stage, ser_rx, h, grs, wq, wo, relay_q, relay_o, near_rx, far_rx, near_own, far_own, qs, heads, totals, out_rx,
    ser_send, ser_recv, gr_send, gr_recv, root_send, relay_recv, swap_send, rl_send, w_recv, fw_send, fw_recv, own_sem,
    near_send, near_recv, far_send, far_recv, out_send, out_recv, credit,
):
    sec = lax.axis_index("section")
    tm = lax.axis_index("tm")
    x, y = sec % 4, sec // 4
    z, c = tm // 2, tm % 2
    is_compute = (x + y) % 2 == 0
    micro = 2 * y + x // 2
    shard = Z * c + z
    sibling = (sec, 2 * z + 1 - c)
    neighbours = (
        4 * y + (x + 1) % 4,
        4 * y + (x + 3) % 4,
        4 * ((y + 1) % 4) + x,
        4 * ((y + 3) % 4) + x,
    )

    def copy(src, dst, send, recv, device):
        return pltpu.make_async_remote_copy(
            src_ref=src, dst_ref=dst, send_sem=send, recv_sem=recv, device_id=device, device_id_type=MESH
        )

    def send_or_keep(src, dst, send, recv, device):
        here = (device[0] == sec) & (device[1] == tm)

        @pl.when(here)
        def _():
            pltpu.make_async_copy(src, dst, recv).start()

        @pl.when(jnp.logical_not(here))
        def _():
            copy(src, dst, send, recv, device).start()

    def sent_unless_kept(src, dst, send, recv, device):
        here = (device[0] == sec) & (device[1] == tm)

        @pl.when(jnp.logical_not(here))
        def _():
            copy(src, dst, send, recv, device).wait_send()

    def near_device(distance):
        other = (shard + distance + 2 * Z) % (2 * Z)
        return (sec, 2 * (other % Z) + other // Z)

    def greet():
        barrier = pltpu.get_barrier_semaphore()

        def meet(device):
            here = (device[0] == sec) & (device[1] == tm)

            @pl.when(jnp.logical_not(here))
            def _():
                pl.semaphore_signal(barrier, inc=1, device_id=device, device_id_type=MESH)

        @pl.loop(0, LAYERS)
        def _(s):
            meet((s, tm))

        @pl.loop(0, 8)
        def _(b):
            meet((compute_section(b), home))

        @pl.when(is_compute)
        def _():
            @pl.loop(0, LAYERS)
            def _(s):
                meet((s, shard))

            meet(sibling)
            for distance in (-1, 1):
                meet(near_device(distance))

        @pl.when(jnp.logical_not(is_compute))
        def _():
            for far in (1, 2):
                meet((sec, 2 * ((z + far) % Z) + c))
                meet((sec, 2 * ((z + Z - far) % Z) + c))

        pl.semaphore_wait(barrier, jnp.where(is_compute, jnp.where(shard == tm, GREET_COMPUTE - 2, GREET_COMPUTE), GREET_RELAY))

    home = 2 * (tm % Z) + tm // Z

    def series_copy(b):
        m = jnp.minimum(b, MICRO - 1)
        return (stage.at[m], ser_rx.at[pl.ds(pl.multiple_of(sec * 64, 64), 64)], ser_send.at[b], ser_recv.at[sec], (compute_section(b), home))

    def gain_copy(b):
        return (gain, grs.at[sec, 0], gr_send.at[b, 0], gr_recv.at[sec, 0], (compute_section(b), tm))

    def readv_copy(b):
        return (readv, grs.at[sec, 1], gr_send.at[b, 1], gr_recv.at[sec, 1], (compute_section(b), tm))

    part = z % 4

    def part_q(step, k):
        return relay_q.at[step, pl.ds(pl.multiple_of(k * 32, 32), 32)]

    def part_o(step, k):
        return relay_o.at[step, pl.ds(pl.multiple_of(k * 16, 16), 16)]

    def part_copies(step, i):
        to = (z + (1, Z - 1, Z + 2 - 4 * c)[i]) % Z
        device = (sec, 2 * to + c)
        return (
            copy(part_q(step, part), part_q(step, part), swap_send.at[step, i, 0], relay_recv.at[step, part, 0], device),
            copy(part_o(step, part), part_o(step, part), swap_send.at[step, i, 1], relay_recv.at[step, part, 1], device),
        )

    def swap_parts(step):
        landed(part_q(step, part), relay_recv.at[step, part, 0])
        landed(part_o(step, part), relay_recv.at[step, part, 1])
        for i in range(3):
            for one in part_copies(step, i):
                one.start()

    def root_copies(w):
        to = relay_section(w)
        e = 4 * c + colour(to)
        device = (to, tm)
        return (
            (wqkv.at[0, pl.ds(pl.multiple_of(e * 128 + part * 32, 32), 32)], part_q(sec, part), root_send.at[w, 0], relay_recv.at[sec, part, 0], device),
            (wout.at[0, pl.ds(pl.multiple_of(e * 64 + part * 16, 16), 16)], part_o(sec, part), root_send.at[w, 1], relay_recv.at[sec, part, 1], device),
        )

    def root_start():
        @pl.loop(0, 8)
        def _(w):
            for args in root_copies(w):
                send_or_keep(*args)

    first_step = jnp.maximum(sec - AHEAD, 0)

    greet()

    @pl.when(first_step == 0)
    def _():
        root_start()

    for m in range(MICRO):
        slot_of = jnp.full((64, ROWS), order[m], jnp.int32)
        picked = series[0].astype(F32)
        for k in range(1, MICRO):
            picked = jnp.where(slot_of == k, series[k].astype(F32), picked)
        stage[m] = picked.astype(BF)

    @pl.loop(0, 8)
    def _(b):
        send_or_keep(*series_copy(b))
        send_or_keep(*gain_copy(b))
        send_or_keep(*readv_copy(b))

    mine = colour(sec)
    eighth = 4 * c + mine

    def relay_copy_q(step, j):
        slot = step % SLOTS
        return copy(relay_q.at[step], wq.at[slot, pl.ds(pl.multiple_of(eighth * 128, 128), 128)], rl_send.at[step, j, 0], w_recv.at[slot, mine, 0], (neighbours[j], tm))

    def relay_copy_o(step, j):
        slot = step % SLOTS
        return copy(relay_o.at[step], wo.at[slot, pl.ds(pl.multiple_of(eighth * 64, 64), 64)], rl_send.at[step, j, 1], w_recv.at[slot, mine, 1], (neighbours[j], tm))

    @pl.when(jnp.logical_not(is_compute))
    def _():
        swap_parts(0)

        @pl.loop(0, LAYERS)
        def _(step):
            @pl.when((step == first_step) & (step > 0))
            def _():
                root_start()

            @pl.when(step >= SLOTS)
            def _():
                for j in range(4):
                    pl.semaphore_wait(credit.at[j], 1)

            for d in range(1, 4):
                k = (part + d) % 4
                landed(part_q(step, k), relay_recv.at[step, k, 0])
                landed(part_o(step, k), relay_recv.at[step, k, 1])
            for j in range(4):

                @pl.when(neighbours[j] != step)
                def _(j=j):
                    relay_copy_q(step, j).start()

            for j in range(4):

                @pl.when(neighbours[j] != step)
                def _(j=j):
                    relay_copy_o(step, j).start()


            @pl.when(step + 1 < LAYERS)
            def _():
                swap_parts(step + 1)

        @pl.loop(0, LAYERS)
        def _(step):
            for j in range(4):

                @pl.when(neighbours[j] != step)
                def _(j=j):
                    relay_copy_q(step, j).wait_send()
                    relay_copy_o(step, j).wait_send()

            for i in range(3):
                for one in part_copies(step, i):
                    one.wait_send()

    def half_copy_q(step):
        slot = step % SLOTS
        half = wq.at[slot, pl.ds(pl.multiple_of(c * 512, 512), 512)]
        return copy(half, half, fw_send.at[slot, 0], fw_recv.at[slot, 0], sibling)

    def half_copy_o(step):
        slot = step % SLOTS
        half = wo.at[slot, pl.ds(pl.multiple_of(c * 256, 256), 256)]
        return copy(half, half, fw_send.at[slot, 1], fw_recv.at[slot, 1], sibling)

    def own_copy(which):
        src, dst = ((wqkv, wq), (wout, wo))[which]
        return pltpu.make_async_copy(src.at[0], dst.at[sec % SLOTS], own_sem.at[which])

    def landed_all(step, which):
        @pl.when(step == sec)
        def _():
            own_copy(which).wait()

        @pl.when(step != sec)
        def _():
            (half_copy_q, half_copy_o)[which](step).wait_recv()

    def share_half(step):
        @pl.when(step == sec)
        def _():
            own_copy(0).start()
            own_copy(1).start()

        @pl.when(step != sec)
        def _():
            share_half_of(step)

    def share_half_of(step):
        slot = step % SLOTS
        for q in range(4):
            e = 4 * c + q
            landed(wq.at[slot, pl.ds(pl.multiple_of(e * 128, 128), 128)], w_recv.at[slot, q, 0])
        half_copy_q(step).start()
        for q in range(4):
            e = 4 * c + q
            landed(wo.at[slot, pl.ds(pl.multiple_of(e * 64, 64), 64)], w_recv.at[slot, q, 1])
        half_copy_o(step).start()

    def near_copy(step, kv):
        return copy(near_own.at[kv], near_rx.at[step, 0, kv], near_send.at[0, kv], near_recv.at[step, 0, kv], near_device(1))

    def near_pass(step, kv):
        return copy(near_rx.at[step, 0, kv], near_rx.at[step, 1, kv], near_send.at[1, kv], near_recv.at[step, 1, kv], near_device(1))

    def far_copy(step):
        return copy(far_own, far_rx.at[step], far_send.at[0], far_recv.at[step], sibling)

    def layer(step):
        slot = step % SLOTS

        @pl.when((step == first_step) & (step > 0))
        def _():
            root_start()

        landed_all(step, 0)
        landed(grs.at[step, 0], gr_recv.at[step, 0])
        hidden = h[...].astype(F32)
        scale = lax.rsqrt(jnp.mean(hidden * hidden, axis=-1, keepdims=True) + EPSILON)
        normed = (hidden * scale * grs[step, 0]).astype(BF)
        near_own[0] = dot(normed, wq[slot, :, 512:768]).astype(BF)
        near_copy(step, 0).start()
        near_own[1] = dot(normed, wq[slot, :, 1024:1280]).astype(BF)
        near_copy(step, 1).start()
        far_own[:, :NEAR] = dot(normed, wq[slot, :, 768:1024]).astype(BF)
        far_own[:, NEAR:] = dot(normed, wq[slot, :, 1280:1536]).astype(BF)
        far_copy(step).start()
        qs[...] = (dot(normed, wq[slot, :, :512]) * (HD**-0.5)).astype(BF)

        row = lax.broadcasted_iota(jnp.int32, (ROWS, ROWS), 0)
        col = lax.broadcasted_iota(jnp.int32, (ROWS, ROWS), 1)
        same = (row < BLK) == (col < BLK)
        far_copy(step).wait_recv()
        block = jnp.where(row < BLK, dil[2 * shard], dil[2 * shard + 1])
        wanted = jnp.where(col < BLK, 0, 1) == block
        for head in range(HEADS):
            k = slice(head * HD, (head + 1) * HD)
            v = slice(NEAR + head * HD, NEAR + (head + 1) * HD)
            q = qs[:, NEAR + head * HD : NEAR + (head + 1) * HD]
            heads[:, NEAR + head * HD : NEAR + (head + 1) * HD] = weighted(
                attend(
                    q,
                    (
                        (far_own[:, k], far_own[:, v], same),
                        (far_rx[step, :, k], far_rx[step, :, v], wanted),
                    ),
                )
            )
        for kv in range(2):
            near_copy(step, kv).wait_recv()
            near_pass(step, kv).start()

        oldest = (col > row) & (shard >= 2)
        middle = (col >= 0) & (shard >= 1)
        begun = []
        for head in range(HEADS):
            k = slice(head * HD, (head + 1) * HD)
            begun.append(
                attend(
                    qs[:, k],
                    (
                        (near_own[0, :, k], near_own[1, :, k], col <= row),
                        (near_rx[step, 0, 0, :, k], near_rx[step, 0, 1, :, k], middle),
                    ),
                )
            )
        @pl.when(step + 1 < LAYERS)
        def _():
            share_half(step + 1)

        for kv in range(2):
            near_pass(step, kv).wait_recv()
        for head in range(HEADS):
            k = slice(head * HD, (head + 1) * HD)
            last = (near_rx[step, 1, 0, :, k], near_rx[step, 1, 1, :, k], oldest)
            heads[:, k] = weighted(attend(qs[:, k], (last,), begun[head]))
        landed_all(step, 1)
        landed(grs.at[step, 1], gr_recv.at[step, 1])
        updated = (h[...].astype(F32) + dot(heads[...], wo[slot])).astype(BF)
        h[...] = updated
        u = updated.astype(F32)
        scale = lax.rsqrt(jnp.mean(u * u, axis=-1, keepdims=True) + EPSILON)
        term = jnp.sum(u * scale * grs[step, 1], axis=-1, keepdims=True)
        totals[...] += jnp.broadcast_to(term, (ROWS, 128))

        for kv in range(2):
            near_copy(step, kv).wait_send()
            near_pass(step, kv).wait_send()
        far_copy(step).wait_send()
        @pl.when(step != sec)
        def _():
            half_copy_q(step).wait_send()
            half_copy_o(step).wait_send()


        @pl.when(step + SLOTS < LAYERS)
        def _():
            for j in range(4):
                pl.semaphore_signal(credit.at[j ^ 1], inc=1, device_id=(neighbours[j], tm), device_id_type=MESH)

    def result_copy(s):
        return (totals.at[pl.ds(pl.multiple_of(8 * s, 8), 8)], out_rx.at[micro], out_send.at[s], out_recv.at[micro], (s, shard))

    @pl.when(is_compute)
    def _():
        totals[...] = jnp.zeros_like(totals)
        for s in range(LAYERS):
            landed(ser_rx.at[pl.ds(s * 64, 64)], ser_recv.at[s])
        for i in range(D // 128):
            block = slice(i * 128, (i + 1) * 128)
            h[:, block] = ser_rx[block, :].astype(F32).T.astype(BF)
        share_half(0)

        @pl.loop(0, LAYERS)
        def _(step):
            layer(step)

        @pl.when(micro < MICRO)
        def _():
            @pl.loop(0, LAYERS)
            def _(s):
                send_or_keep(*result_copy(s))

    lane = lax.broadcasted_iota(jnp.int32, (8, 128), 1)
    line = lax.broadcasted_iota(jnp.int32, (8, 128), 0)
    for m in range(MICRO):
        landed(out_rx.at[m], out_recv.at[m])
        turned = jnp.sum(jnp.where(lane == line, out_rx[m], 0.0), axis=0, keepdims=True)
        out[m] = turned[:, :8]

    @pl.when(is_compute & (micro < MICRO))
    def _():
        @pl.loop(0, LAYERS)
        def _(s):
            sent_unless_kept(*result_copy(s))

    @pl.loop(0, 8)
    def _(b):
        sent_unless_kept(*series_copy(b))
        sent_unless_kept(*gain_copy(b))
        sent_unless_kept(*readv_copy(b))
        for args in root_copies(b):
            sent_unless_kept(*args)


def local(series, query_key_value_weight, output_weight, gain, readout_weight, dilation_block, order):
    dma = pltpu.SemaphoreType.DMA
    vmem = pl.BlockSpec(memory_space=pltpu.VMEM)
    hbm = pl.BlockSpec(memory_space=pl.ANY)
    smem = pl.BlockSpec(memory_space=pltpu.SMEM)
    return pl.pallas_call(
        kernel,
        out_shape=jax.ShapeDtypeStruct((MICRO, 1, 8), F32),
        in_specs=[vmem, hbm, hbm, vmem, vmem, smem, smem],
        out_specs=vmem,
        scratch_shapes=[
            pltpu.VMEM((MICRO, 64, ROWS), BF),
            pltpu.VMEM((D, ROWS), BF),
            pltpu.VMEM((ROWS, D), BF),
            pltpu.VMEM((LAYERS, 2, 1, D), F32),
            pltpu.VMEM((SLOTS, D, 1536), BF),
            pltpu.VMEM((SLOTS, 512, D), BF),
            pltpu.VMEM((LAYERS, 128, 1536), BF),
            pltpu.VMEM((LAYERS, 64, D), BF),
            pltpu.VMEM((LAYERS, 2, 2, ROWS, NEAR), BF),
            pltpu.VMEM((LAYERS, ROWS, 2 * NEAR), BF),
            pltpu.VMEM((2, ROWS, NEAR), BF),
            pltpu.VMEM((ROWS, 2 * NEAR), BF),
            pltpu.VMEM((ROWS, 512), BF),
            pltpu.VMEM((ROWS, 512), BF),
            pltpu.VMEM((ROWS, 128), F32),
            pltpu.VMEM((MICRO, 8, 128), F32),
            dma((8,)), dma((LAYERS,)),
            dma((8, 2)), dma((LAYERS, 2)),
            dma((8, 2)), dma((LAYERS, 4, 2)), dma((LAYERS, 3, 2)),
            dma((LAYERS, 4, 2)), dma((SLOTS, 4, 2)),
            dma((SLOTS, 2)), dma((SLOTS, 2)), dma((2,)),
            dma((2, 2)), dma((LAYERS, 2, 2)),
            dma((1,)), dma((LAYERS,)),
            dma((LAYERS,)), dma((MICRO,)),
            pltpu.SemaphoreType.REGULAR((4,)),
        ],
        compiler_params=pltpu.CompilerParams(collective_id=0, has_side_effects=True, vmem_limit_bytes=58 * 2**20),
    )(jnp.swapaxes(series, 1, 2), query_key_value_weight, output_weight, gain, readout_weight, dilation_block, order)


def solution(mesh):
    placed = (
        P(None, "tm", "section"),
        P("section", None, None),
        P("section", None, None),
        P("section", None),
        P("section", None),
        P(),
        P(),
    )
    return jax.shard_map(
        local, mesh=mesh, in_specs=placed, out_specs=P(None, "tm", "section"), check_vma=False
    )
```
